32 devices in a mesh: groups: 2 (over y), field: 4 (over x, core), wave: 4 (over z).
Axes of the slice: x: 2, y: 2, z: 4, core: 2. Of those that a mesh axis runs over, the one named last changes fastest.
Arguments:
- mode_basis: bfloat16 [22, 512, 512], P(None, 'wave'), may hold values from -6 to 6
- coef_table: bfloat16 [4096, 22], replicated, may hold values from -1.5 to 1.5
- table_index: int32 [64], P(('groups', 'field')), parts along dimension 0, may hold values from 0 to 4095
- wave_lengths: float32 [8], P('wave'), may hold values from 0.32 to 1.05
- sed_table: float32 [1024, 8], replicated, may hold values from 0.05 to 1
- template_ids: int32 [64, 8], P(('groups', 'field')), parts along dimension 0, may hold values from 0 to 1023
Outputs:
- mixed: bfloat16 [64, 8, 256, 256], P(('groups', 'field'), None, 'wave'), parts along dimension 0
The draws below stay inside these ranges and needn't reach their ends.
There are 2 independent parts, one for each index of `groups`. The reference program is written for one: setup_inputs(seed, part) draws one part's arguments, and reference() takes and returns one part's arrays. A program takes and returns all parts, laid end to end along the dimension named above; an argument that names none is the same for every part. Nothing has to cross between parts.
All inputs are finite; a program needn't handle non-finite values.
Results may differ from the reference program's by a relative error of at most 0.0065.
Values may be sent and summed in bfloat16 or wider, within the bound.
A program may use at most 128 MiB of HBM per device.

```python
import math
import jax
import jax.numpy as jnp
from jax import lax

PUP = 512
PIX = 256
K = 22
NTAB = 4096
NSED = 1024
J = 8
F = 32
W = 8


def with_ends(values, rng, least, largest):
    longest = values.shape.index(max(values.shape))
    spots = []
    for shift in (0, 1):
        where = [jax.random.randint(jax.random.fold_in(rng, axis), (), 0, length) for axis, length in enumerate(values.shape)]
        where[longest] = (where[longest] + shift) % values.shape[longest]
        spots.append(tuple(where))
    return values.at[spots[0]].set(least).at[spots[1]].set(largest)


def levels(key, extent, pieces, least, largest):
    level = 1.0
    for position, shards_of in pieces:
        steps = jax.random.uniform(jax.random.fold_in(jax.random.fold_in(key, 6), position), (shards_of,), jnp.float32, least / len(pieces), largest / len(pieces))
        level = level * jnp.repeat(jnp.exp(steps), extent[position] // shards_of).reshape((-1,) + (1,) * (len(extent) - 1 - position))
    return level


def gaussian(own_key, shape, deviation, reach, shards=(), held_as=jnp.bfloat16):
    array = jax.random.normal(own_key, shape, jnp.float32) * deviation
    if len(shards) > 0:
        array = levels(own_key, shape, shards, -0.22, 0.18) * array
    return jnp.clip(array, min=-reach, max=reach).astype(held_as)


def setup_inputs(seed: int = 0, part: int = 0) -> dict:
    key_list = jax.random.split(jax.random.key(seed), 7)
    part_keys = jax.random.split(jax.random.fold_in(key_list[6], part), 7)
    mode_basis = gaussian(key_list[0], (K, PUP, PUP), 1.0, 6.0, ((1, 4),))
    coef_table = gaussian(key_list[1], (NTAB, K), 0.25, 1.5)
    table_index = with_ends(jax.random.randint(part_keys[2], (F,), 0, NTAB), jax.random.fold_in(part_keys[2], 1), 0, NTAB - 1).astype(jnp.int32)
    wave_lengths = jnp.clip(jnp.exp(math.log(1.05) - 1.1882244 * jax.random.uniform(key_list[3], (W,), jnp.float32) ** levels(key_list[3], (W,), ((0, 4),), -0.2, 0.2)), 0.32, 1.05)
    sed_table = jnp.clip(jnp.exp(jax.random.uniform(key_list[4], (NSED, W), jnp.float32, math.log(0.05), math.log(1.0))), 0.05, 1.0)
    template_ids = with_ends(jax.random.randint(part_keys[5], (F, J), 0, NSED), jax.random.fold_in(part_keys[5], 1), 0, NSED - 1).astype(jnp.int32)
    return dict(mode_basis=mode_basis, coef_table=coef_table, table_index=table_index, wave_lengths=wave_lengths, sed_table=sed_table, template_ids=template_ids)


TWO_PI = 2.0 * math.pi
SAMPLING = 0.25
EPSILON = 1e-6


def transform_table(wave_lengths, pixels, pupil_side):
    pixel_offset = jnp.arange(pixels, dtype=jnp.int32) - pixels // 2
    pupil_offset = 2 * jnp.arange(pupil_side, dtype=jnp.int32) - pupil_side + 1
    products = (pixel_offset[:, None] * pupil_offset[None, :]).astype(jnp.float32)
    factor = (TWO_PI * SAMPLING / (2.0 * pupil_side)) / wave_lengths
    angles = products[None, :, :] * factor[:, None, None]
    cosine = jnp.cos(angles)
    sine_part = jnp.sin(angles)
    upper_half = jnp.concatenate([cosine, sine_part], axis=2)
    lower_half = jnp.concatenate([-sine_part, cosine], axis=2)
    return jnp.concatenate([upper_half, lower_half], axis=1).astype(jnp.bfloat16)


def aperture_rows(row_start, row_count, pupil_side):
    row_pos = 2 * (row_start + jnp.arange(row_count, dtype=jnp.int32)) - pupil_side + 1
    col_pos = 2 * jnp.arange(pupil_side, dtype=jnp.int32) - pupil_side + 1
    radius_sq = row_pos[:, None] * row_pos[:, None] + col_pos[None, :] * col_pos[None, :]
    inner_edge = (61 * pupil_side) // 100
    inside = (radius_sq <= pupil_side * pupil_side) & (radius_sq >= inner_edge * inner_edge)
    return inside.astype(jnp.float32)


def pupil_section(path_rows, wave_lengths, kernel_table):
    row_count = path_rows.shape[1]
    pupil_side = path_rows.shape[2]
    opening = aperture_rows(0, row_count, pupil_side)
    phase_map = path_rows[:, None, :, :] * (TWO_PI / wave_lengths)[None, :, None, None]
    field_real = opening * jnp.cos(phase_map)
    field_imag = opening * jnp.sin(phase_map)
    pupil_field = jnp.concatenate([field_real, field_imag], axis=3).astype(jnp.bfloat16)
    first_pass = jnp.einsum("flxy,luy->flxu", pupil_field.astype(jnp.float32), kernel_table.astype(jnp.float32))
    return first_pass.astype(jnp.bfloat16)


def finish_section(first_pass, kernel_table):
    pixels = first_pass.shape[3] // 2
    stacked = jnp.concatenate([first_pass[..., :pixels], first_pass[..., pixels:]], axis=2)
    image_field = jnp.einsum("lux,flxv->fluv", kernel_table.astype(jnp.float32), stacked.astype(jnp.float32))
    intensity = image_field[:, :, :pixels] * image_field[:, :, :pixels] + image_field[:, :, pixels:] * image_field[:, :, pixels:]
    mean_level = jnp.mean(intensity, axis=(2, 3), keepdims=True)
    return (intensity / (mean_level + EPSILON)).astype(jnp.bfloat16)


def reference(mode_basis, coef_table, table_index, wave_lengths, sed_table, template_ids):
    kernel_table = transform_table(wave_lengths, PIX, PUP)
    flat_basis = mode_basis.reshape(K, PUP * PUP)

    def one_position(inputs):
        index_value, id_row = inputs
        coeffs = coef_table[index_value]
        path_diff = jnp.dot(coeffs[None, :], flat_basis, preferred_element_type=jnp.float32).reshape(1, PUP, PUP)
        first_pass = pupil_section(path_diff, wave_lengths, kernel_table)
        spectra = finish_section(first_pass, kernel_table)
        raw_weights = sed_table[id_row]
        weights = (raw_weights / jnp.sum(raw_weights, axis=1, keepdims=True)).astype(jnp.bfloat16)
        mixed = jnp.einsum("jl,lrp->jrp", weights.astype(jnp.float32), spectra[0].astype(jnp.float32))
        return mixed.astype(jnp.bfloat16)

    return lax.map(one_position, (table_index, template_ids))
```

```python
import functools

import jax
import jax.numpy as jnp
from jax import lax
from jax.experimental import pallas as pl
from jax.experimental.pallas import tpu as pltpu
from jax.sharding import PartitionSpec as P

PUP = 512
PIX = 256
EPSILON = 1e-06
GROUP = 16
ROUNDER = 12582912.0


def turns_sincos(turns):
    nearest = (turns + ROUNDER) - ROUNDER
    r = turns - nearest
    s = r * r
    a = r * SINE(s)
    b = COSINE(s)
    return 1.0 - a * a, a * b


def SINE(s):
    return SIN[0] + s * (SIN[1] + s * (SIN[2] + s * SIN[3]))


def COSINE(s):
    return COS[0] + s * (COS[1] + s * (COS[2] + s * (COS[3] + s * COS[4])))


SIN = (4.442879676818848, -7.307816505432129, 3.5977742671966553, -0.7911993861198425)
COS = (1.4142135381698608, -6.978850841522217, 5.739460468292236, -1.883557915687561, 0.3106880187988281)


def transform_kernel(
    waves, fields, inv_ref, mix_ref, basis_ref, power_ref, total_ref, path, image, opening, table, efield
):
    slab = pl.program_id(0)
    slabs = pl.num_programs(0)
    rows = basis_ref.shape[3]
    modes = basis_ref.shape[0] * basis_ref.shape[2]
    upix = power_ref.shape[1] // fields
    first_row = slab * rows
    first_pix = lax.axis_index("wave") * upix

    x = 2 * (first_row + lax.broadcasted_iota(jnp.int32, (rows, PUP), 0)) - PUP + 1
    y = 2 * lax.broadcasted_iota(jnp.int32, (rows, PUP), 1) - PUP + 1
    radius = x * x + y * y
    inner = 61 * PUP // 100
    inside = (radius <= PUP * PUP) & (radius >= inner * inner)
    opening[...] = inside.astype(jnp.float32).astype(jnp.bfloat16)

    for r in range(0, rows, GROUP):
        block = basis_ref[:, 0, :, r : r + GROUP, :].reshape(modes * GROUP, PUP)
        diff = jnp.dot(mix_ref[...], block, preferred_element_type=jnp.float32)
        path[:, r : r + GROUP, :] = diff.reshape(fields, GROUP, PUP)

    def pass_wave(wave, first):
        inv = inv_ref[wave]
        scale = inv * (0.25 / (2.0 * PUP))
        lane = lax.broadcasted_iota(jnp.int32, (upix, 2 * rows), 1)
        real = lane < rows
        xs = 2 * (first_row + jnp.where(real, lane, lane - rows)) - PUP + 1
        us = first_pix + lax.broadcasted_iota(jnp.int32, (upix, 2 * rows), 0) - PIX // 2
        cosine, sine = turns_sincos((us * xs).astype(jnp.float32) * scale)
        kernel = jnp.concatenate(
            [jnp.where(real, cosine, sine), jnp.where(real, -sine, cosine)], axis=0
        ).astype(jnp.bfloat16)
        for f in range(fields):
            slot = f % 2
            for r in range(0, rows, GROUP):
                cosine, sine = turns_sincos(path[f, r : r + GROUP, :] * inv)
                hole = opening[r : r + GROUP, :]
                efield[slot, r : r + GROUP, :] = cosine.astype(jnp.bfloat16) * hole
                efield[slot, rows + r : rows + r + GROUP, :] = sine.astype(jnp.bfloat16) * hole
            part = jnp.dot(kernel, efield[slot], preferred_element_type=jnp.float32)
            here = pl.ds(f * upix, upix)
            if first:
                image[wave, here, :PUP] = part[:upix]
                image[wave, here, PUP:] = part[upix:]
            else:
                image[wave, here, :PUP] += part[:upix]
                image[wave, here, PUP:] += part[upix:]

    @pl.when(slab == 0)
    def _():
        lax.fori_loop(0, waves, lambda l, c: (pass_wave(l, True), c)[1], 0)

    @pl.when(slab > 0)
    def _():
        lax.fori_loop(0, waves, lambda l, c: (pass_wave(l, False), c)[1], 0)

    @pl.when(slab == slabs - 1)
    def _():
        def finish(wave, carry):
            scale = inv_ref[wave] * (0.25 / (2.0 * PUP))
            step = 64
            for r in range(0, PUP, step):
                ys = 2 * (r + lax.broadcasted_iota(jnp.int32, (step, PIX), 0)) - PUP + 1
                vs = lax.broadcasted_iota(jnp.int32, (step, PIX), 1) - PIX // 2
                cosine, sine = turns_sincos((ys * vs).astype(jnp.float32) * scale)
                cosine = cosine.astype(jnp.bfloat16)
                table[r : r + step, :PIX] = cosine
                table[r : r + step, PIX:] = (-sine).astype(jnp.bfloat16)
                table[PUP + r : PUP + r + step, :PIX] = sine.astype(jnp.bfloat16)
                table[PUP + r : PUP + r + step, PIX:] = cosine
            half = fields * upix // 2
            for h in range(2):
                field = jnp.dot(
                    image[wave, h * half : (h + 1) * half, :].astype(jnp.bfloat16),
                    table[...],
                    preferred_element_type=jnp.float32,
                )
                re, im = field[:, :PIX], field[:, PIX:]
                power = re * re + im * im
                power_ref[wave, h * half : (h + 1) * half, :] = power
                sums = jnp.sum(power.reshape(fields // 2, upix, PIX), axis=1)
                total_ref[wave, h * (fields // 2) : (h + 1) * (fields // 2), :] = sums
            return carry

        lax.fori_loop(0, waves, finish, 0)


def mix_kernel(fields, power_ref, level_ref, weight_ref, out_ref):
    f = pl.program_id(0)
    waves = power_ref.shape[0]
    templates = out_ref.shape[1]
    step = 16
    for r in range(0, power_ref.shape[1], step):
        sums = [None] * templates
        for l in range(waves):
            spectrum = (power_ref[l, r : r + step, :] * level_ref[l * fields + f]).astype(jnp.bfloat16)
            spectrum = spectrum.astype(jnp.float32)
            for j in range(templates):
                term = spectrum * weight_ref[(f * templates + j) * waves + l]
                sums[j] = term if l == 0 else sums[j] + term
        for j in range(templates):
            out_ref[0, j, r : r + step, :] = sums[j].astype(jnp.bfloat16)


def local(sizes, mode_basis, coef_table, table_index, wave_lengths, sed_table, template_ids):
    slabs, field_parts, group_parts = sizes
    count, rows, _ = mode_basis.shape
    fields = table_index.shape[0]
    upix = PIX // slabs
    plane = field_parts * group_parts
    own = -(-count // plane)
    inverse = 1.0 / lax.all_gather(wave_lengths, "wave", axis=0, tiled=True)
    waves = inverse.shape[0]

    place = lax.axis_index("groups") * field_parts + lax.axis_index("field")
    padded = jnp.pad(mode_basis, ((0, plane * own - count), (0, 0), (0, 0)))
    piece = lax.dynamic_slice_in_dim(padded, place * own, own, 0)
    column = lax.all_gather(piece, "wave", axis=0)
    basis = lax.all_gather(column, ("groups", "field"), axis=0)

    coeffs = jnp.pad(jnp.take(coef_table, table_index, axis=0, mode="clip"), ((0, 0), (0, plane * own - count)))
    same = jnp.eye(GROUP, dtype=jnp.bfloat16)
    mix = (coeffs[:, None, :, None] * same[None, :, None, :]).reshape(fields * GROUP, -1)

    power, total = pl.pallas_call(
        functools.partial(transform_kernel, waves, fields),
        grid=(slabs,),
        in_specs=[
            pl.BlockSpec(memory_space=pltpu.SMEM),
            pl.BlockSpec(memory_space=pltpu.VMEM),
            pl.BlockSpec((plane, 1, own, rows, PUP), lambda s: (0, s, 0, 0, 0)),
        ],
        out_specs=[
            pl.BlockSpec((waves, fields * upix, PIX), lambda s: (0, 0, 0)),
            pl.BlockSpec((waves, fields, PIX), lambda s: (0, 0, 0)),
        ],
        out_shape=[
            jax.ShapeDtypeStruct((waves, fields * upix, PIX), jnp.float32),
            jax.ShapeDtypeStruct((waves, fields, PIX), jnp.float32),
        ],
        scratch_shapes=[
            pltpu.VMEM((fields, rows, PUP), jnp.float32),
            pltpu.VMEM((waves, fields * upix, 2 * PUP), jnp.float32),
            pltpu.VMEM((rows, PUP), jnp.bfloat16),
            pltpu.VMEM((2 * PUP, 2 * PIX), jnp.bfloat16),
            pltpu.VMEM((2, 2 * rows, PUP), jnp.bfloat16),
        ],
        compiler_params=pltpu.CompilerParams(vmem_limit_bytes=56 * 2**20),
    )(inverse, mix, basis)

    mean = lax.psum(jnp.sum(total, axis=2), "wave") / (PIX * PIX)
    level = (1.0 / (mean + EPSILON)).reshape(-1)
    raw = jnp.take(sed_table, template_ids, axis=0, mode="clip")
    weights = (raw / jnp.sum(raw, axis=2, keepdims=True)).astype(jnp.bfloat16).astype(jnp.float32)
    templates = template_ids.shape[1]
    return pl.pallas_call(
        functools.partial(mix_kernel, fields),
        grid=(fields,),
        in_specs=[
            pl.BlockSpec((waves, upix, PIX), lambda f: (0, f, 0)),
            pl.BlockSpec(memory_space=pltpu.SMEM),
            pl.BlockSpec(memory_space=pltpu.SMEM),
        ],
        out_specs=pl.BlockSpec((1, templates, upix, PIX), lambda f: (f, 0, 0, 0)),
        out_shape=jax.ShapeDtypeStruct((fields, templates, upix, PIX), jnp.bfloat16),
    )(power, level, weights.reshape(-1))


def solution(mesh):
    sizes = (mesh.shape["wave"], mesh.shape["field"], mesh.shape["groups"])
    return jax.shard_map(
        functools.partial(local, sizes),
        mesh=mesh,
        in_specs=(
            P(None, "wave", None),
            P(),
            P(("groups", "field")),
            P("wave"),
            P(),
            P(("groups", "field"), None),
        ),
        out_specs=P(("groups", "field"), None, "wave", None),
        check_vma=False,
    )
```

```python
import functools

import jax
import jax.numpy as jnp
from jax import lax
from jax.experimental import pallas as pl
from jax.experimental.pallas import tpu as pltpu
from jax.sharding import PartitionSpec as P

PUP = 512
PIX = 256
EPSILON = 1e-06
GROUP = 16
ROUNDER = 12582912.0


def turns_sincos(turns):
    nearest = (turns + ROUNDER) - ROUNDER
    r = turns - nearest
    s = r * r
    a = r * SINE(s)
    b = COSINE(s)
    return 1.0 - a * a, a * b


def SINE(s):
    return SIN[0] + s * (SIN[1] + s * (SIN[2] + s * SIN[3]))


def COSINE(s):
    return COS[0] + s * (COS[1] + s * (COS[2] + s * (COS[3] + s * COS[4])))


SIN = (4.442879676818848, -7.307816505432129, 3.5977742671966553, -0.7911993861198425)
COS = (1.4142135381698608, -6.978850841522217, 5.739460468292236, -1.883557915687561, 0.3106880187988281)


def hop(order, slabs):
    odd = order % 2
    return odd * ((order + 1) // 2) + (1 - odd) * (slabs - order // 2)


def psf_kernel(
    sizes, waves, fields, mix_ref, weight_ref, length_ref, basis_ref, out_ref,
    whole, inverse, path, image, table, efield, power, total, arrived,
    local_sem, wl_send, wl_recv, send1, recv1, send2, recv2, send3, recv3, sum_send, sum_recv,
):
    slabs, field_parts, group_parts = sizes
    count, rows, _ = basis_ref.shape
    modes = whole.shape[1]
    upix = PIX // slabs
    own_waves = waves // slabs
    x_parts = field_parts // 2
    chips = x_parts * group_parts
    own = modes // (2 * chips)
    templates = out_ref.shape[1]

    me = lax.axis_index("wave")
    part = lax.axis_index("field")
    core = part % 2
    chip = lax.axis_index("groups") * x_parts + part // 2
    first_pix = me * upix

    def wave_peer(shift):
        return {"wave": (me + shift) % slabs}

    def chip_peer(shift):
        other = (chip + shift) % chips
        return {"groups": other // x_parts, "field": (other % x_parts) * 2 + core}

    sibling = {"field": part + 1 - 2 * core}

    def remote(src, dst, send, recv, device):
        return pltpu.make_async_remote_copy(
            src_ref=src, dst_ref=dst, send_sem=send, recv_sem=recv,
            device_id=device, device_id_type=pl.DeviceIdType.MESH,
        )

    def from_slab(order):
        return (me + 2 * slabs - hop(order, slabs)) % slabs

    def piece(slab, of_chip):
        return whole.at[slab, pl.ds((core * chips + of_chip) * own, own)]

    def first_copy(order):
        shift = hop(order, slabs)
        mine = piece(me, chip)
        return remote(mine, mine, send1.at[order - 1], recv1.at[order - 1], wave_peer(shift))

    def first_landed(order):
        ref = piece(from_slab(order), chip)
        return remote(ref, ref, send1.at[order - 1], recv1.at[order - 1], wave_peer(hop(order, slabs)))

    def plane_copy(order, shift):
        ref = piece(from_slab(order), chip)
        at = (order - 1, shift - 1)
        return remote(ref, ref, send2.at[at], recv2.at[at], chip_peer(shift))

    def plane_landed(order, shift):
        ref = piece(from_slab(order), (chip + chips - shift) % chips)
        at = (order - 1, shift - 1)
        return remote(ref, ref, send2.at[at], recv2.at[at], chip_peer(shift))

    def core_copy(order, which):
        ref = whole.at[from_slab(order), pl.ds(which * chips * own, chips * own)]
        return remote(ref, ref, send3.at[order - 1], recv3.at[order - 1], sibling)

    def length_copy(shift, sender):
        ref = inverse.at[pl.ds(sender * own_waves, own_waves)]
        return remote(ref, ref, wl_send.at[shift - 1], wl_recv.at[shift - 1], wave_peer(shift))

    barrier = pltpu.get_barrier_semaphore()
    peers = [wave_peer(d) for d in range(1, slabs)] + [chip_peer(e) for e in range(1, chips)] + [sibling]
    for peer in peers:
        pl.semaphore_signal(barrier, inc=1, device_id=peer, device_id_type=pl.DeviceIdType.MESH)
    bring = pltpu.make_async_copy(basis_ref, whole.at[me, pl.ds(0, count)], local_sem)
    bring.start()
    if modes > count:
        whole[me, count:, :, :] = jnp.zeros((modes - count, rows, PUP), jnp.bfloat16)
    inverse[pl.ds(me * own_waves, own_waves)] = 1.0 / length_ref[...]
    pl.semaphore_wait(barrier, len(peers))
    for d in range(1, slabs):
        length_copy(d, me).start()
    bring.wait()
    first_copy(1).start()

    def clear(f, carry):
        for l in range(waves):
            image[l, pl.ds(f * upix, upix), :] = jnp.zeros((upix, 2 * PUP), jnp.float32)
        return carry

    lax.fori_loop(0, fields, clear, 0)
    for d in range(1, slabs):
        length_copy(d, (me + slabs - d) % slabs).wait_recv()

    def step_body(step, carry):
        order = step // waves
        wave = step % waves
        slab = from_slab(order)
        first_row = slab * rows

        for o in range(1, slabs):

            @pl.when(step == (o * 7 * waves) // 16)
            def _():
                first_landed(o).wait_recv()
                if o + 1 < slabs:
                    first_copy(o).wait_send()
                    first_copy(o + 1).start()
                for e in range(1, chips):
                    plane_copy(o, e).start()

            @pl.when(step == (o * waves - waves // 2 if o > 1 else waves))
            def _():
                for e in range(1, chips):
                    plane_landed(o, e).wait_recv()
                core_copy(o, core).start()

            @pl.when(step == o * waves)
            def _():
                core_copy(o, 1 - core).wait_recv()

        @pl.when(wave == 0)
        def _():
            def paths(g, c):
                r = pl.multiple_of(g * GROUP, GROUP)
                block = whole[slab, :, pl.ds(r, GROUP), :].reshape(modes * GROUP, PUP)
                diff = jnp.dot(mix_ref[...], block, preferred_element_type=jnp.float32)
                path[:, pl.ds(r, GROUP), :] = diff.reshape(fields, GROUP, PUP)
                x = 2 * (first_row + r + lax.broadcasted_iota(jnp.int32, (GROUP, PUP), 0)) - PUP + 1
                y = 2 * lax.broadcasted_iota(jnp.int32, (GROUP, PUP), 1) - PUP + 1
                radius = x * x + y * y
                inner = 61 * PUP // 100
                inside = (radius <= PUP * PUP) & (radius >= inner * inner)
                efield[2, pl.ds(r, GROUP), :] = inside.astype(jnp.float32).astype(jnp.bfloat16)
                return c

            lax.fori_loop(0, rows // GROUP, paths, 0)

        inv = inverse[wave]
        lane = lax.broadcasted_iota(jnp.int32, (upix, 2 * rows), 1)
        real = lane < rows
        xs = 2 * (first_row + jnp.where(real, lane, lane - rows)) - PUP + 1
        us = first_pix + lax.broadcasted_iota(jnp.int32, (upix, 2 * rows), 0) - PIX // 2
        scale = inv[:1, : 2 * rows] * (0.25 / (2.0 * PUP))
        cosine, sine = turns_sincos((us * xs).astype(jnp.float32) * scale)
        kernel = jnp.concatenate(
            [jnp.where(real, cosine, sine), jnp.where(real, -sine, cosine)], axis=0
        ).astype(jnp.bfloat16)
        for f in range(fields):
            slot = f % 2
            for r in range(0, rows, GROUP):
                cosine, sine = turns_sincos(path[f, r : r + GROUP, :] * inv[:1])
                hole = efield[2, r : r + GROUP, :]
                efield[slot, r : r + GROUP, :] = cosine.astype(jnp.bfloat16) * hole
                efield[slot, rows + r : rows + r + GROUP, :] = sine.astype(jnp.bfloat16) * hole
            part_sum = jnp.dot(kernel, efield[slot], preferred_element_type=jnp.float32)
            here = pl.ds(f * upix, upix)
            image[wave, here, :PUP] += part_sum[:upix]
            image[wave, here, PUP:] += part_sum[upix:]
        return carry

    lax.fori_loop(0, slabs * waves, step_body, 0)

    def finish(wave, carry):
        scale = inverse[wave][:1, :PIX] * (0.25 / (2.0 * PUP))
        step = 64
        for r in range(0, PUP, step):
            ys = 2 * (r + lax.broadcasted_iota(jnp.int32, (step, PIX), 0)) - PUP + 1
            vs = lax.broadcasted_iota(jnp.int32, (step, PIX), 1) - PIX // 2
            cosine, sine = turns_sincos((ys * vs).astype(jnp.float32) * scale)
            cosine = cosine.astype(jnp.bfloat16)
            table[r : r + step, :PIX] = cosine
            table[r : r + step, PIX:] = (-sine).astype(jnp.bfloat16)
            table[PUP + r : PUP + r + step, :PIX] = sine.astype(jnp.bfloat16)
            table[PUP + r : PUP + r + step, PIX:] = cosine
        half = fields * upix // 2
        for h in range(2):
            field = jnp.dot(
                image[wave, h * half : (h + 1) * half, :].astype(jnp.bfloat16),
                table[...],
                preferred_element_type=jnp.float32,
            )
            re, im = field[:, :PIX], field[:, PIX:]
            bright = re * re + im * im
            power[wave, h * half : (h + 1) * half, :] = bright
            sums = jnp.sum(jnp.sum(bright.reshape(fields // 2, upix, PIX), axis=1), axis=1, keepdims=True)
            total[wave, h * (fields // 2) : (h + 1) * (fields // 2), :] = jnp.broadcast_to(
                sums, (fields // 2, PIX)
            )
        return carry

    lax.fori_loop(0, waves, finish, 0)

    def sum_copy(shift):
        return remote(
            total, arrived.at[shift - 1], sum_send.at[shift - 1], sum_recv.at[shift - 1], wave_peer(shift)
        )

    for d in range(1, slabs):
        sum_copy(d).start()
    for d in range(1, slabs):
        sum_copy(d).wait()
    everything = total[...]
    for d in range(1, slabs):
        everything = everything + arrived[d - 1]
    total[...] = 1.0 / (everything * (1.0 / (PIX * PIX)) + EPSILON)

    step = 16

    def mix_fields(f, carry):
        for r in range(0, upix, step):
            sums = [None] * templates
            for l in range(waves):
                level = total[l, pl.ds(f, 1), :]
                bright = power[l, pl.ds(pl.multiple_of(f * upix, step) + r, step), :]
                spectrum = (bright * level).astype(jnp.bfloat16).astype(jnp.float32)
                for j in range(templates):
                    term = spectrum * weight_ref[(f * templates + j) * waves + l]
                    sums[j] = term if l == 0 else sums[j] + term
            for j in range(templates):
                out_ref[f, j, r : r + step, :] = sums[j].astype(jnp.bfloat16)
        return carry

    lax.fori_loop(0, fields, mix_fields, 0)

    for d in range(1, slabs):
        length_copy(d, me).wait_send()
    first_copy(slabs - 1).wait_send()
    for o in range(1, slabs):
        for e in range(1, chips):
            plane_copy(o, e).wait_send()
        core_copy(o, core).wait_send()


def local(sizes, waves, mode_basis, coef_table, table_index, wave_lengths, sed_table, template_ids):
    slabs, field_parts, group_parts = sizes
    count, rows, _ = mode_basis.shape
    fields, templates = template_ids.shape
    upix = PIX // slabs
    plane = field_parts * group_parts
    chips = plane // 2
    own = -(-count // plane)
    modes = plane * own

    coeffs = jnp.take(coef_table, table_index, axis=0, mode="clip")
    coeffs = jnp.pad(coeffs, ((0, 0), (0, modes - count)))
    same = jnp.eye(GROUP, dtype=jnp.bfloat16)
    mix = (coeffs[:, None, :, None] * same[None, :, None, :]).reshape(fields * GROUP, -1)
    raw = jnp.take(sed_table, template_ids, axis=0, mode="clip")
    weights = (raw / jnp.sum(raw, axis=2, keepdims=True)).astype(jnp.bfloat16).astype(jnp.float32)
    lengths = jnp.broadcast_to(wave_lengths[:, None, None], (wave_lengths.shape[0], 8, PUP))
    hops = slabs - 1
    dma = pltpu.SemaphoreType.DMA

    return pl.pallas_call(
        functools.partial(psf_kernel, sizes, waves, fields),
        in_specs=[
            pl.BlockSpec(memory_space=pltpu.VMEM),
            pl.BlockSpec(memory_space=pltpu.SMEM),
            pl.BlockSpec(memory_space=pltpu.VMEM),
            pl.BlockSpec(memory_space=pl.ANY),
        ],
        out_specs=pl.BlockSpec(memory_space=pltpu.VMEM),
        out_shape=jax.ShapeDtypeStruct((fields, templates, upix, PIX), jnp.bfloat16),
        scratch_shapes=[
            pltpu.VMEM((slabs, modes, rows, PUP), jnp.bfloat16),
            pltpu.VMEM((waves, 8, PUP), jnp.float32),
            pltpu.VMEM((fields, rows, PUP), jnp.float32),
            pltpu.VMEM((waves, fields * upix, 2 * PUP), jnp.float32),
            pltpu.VMEM((2 * PUP, 2 * PIX), jnp.bfloat16),
            pltpu.VMEM((3, 2 * rows, PUP), jnp.bfloat16),
            pltpu.VMEM((waves, fields * upix, PIX), jnp.float32),
            pltpu.VMEM((waves, fields, PIX), jnp.float32),
            pltpu.VMEM((hops, waves, fields, PIX), jnp.float32),
            dma,
            dma((hops,)),
            dma((hops,)),
            dma((hops,)),
            dma((hops,)),
            dma((hops, chips - 1)),
            dma((hops, chips - 1)),
            dma((hops,)),
            dma((hops,)),
            dma((hops,)),
            dma((hops,)),
        ],
        compiler_params=pltpu.CompilerParams(
            vmem_limit_bytes=60 * 2**20, collective_id=0, has_side_effects=True
        ),
    )(mix, weights.reshape(-1), lengths, mode_basis)


def solution(mesh):
    sizes = (mesh.shape["wave"], mesh.shape["field"], mesh.shape["groups"])


    def whole_program(*args):
        return sharded(mesh, functools.partial(local, sizes, args[3].shape[0]))(*args)

    return whole_program


def sharded(mesh, body):
    return jax.shard_map(
        body,
        mesh=mesh,
        in_specs=(
            P(None, "wave", None),
            P(),
            P(("groups", "field")),
            P("wave"),
            P(),
            P(("groups", "field"), None),
        ),
        out_specs=P(("groups", "field"), None, "wave", None),
        check_vma=False,
    )
```
